32 devices in a mesh: sample: 4 (over y, x), row: 2 (over core), col: 4 (over z).
Axes of the slice: x: 2, y: 2, z: 4, core: 2. Of those that a mesh axis runs over, the one named last changes fastest.
Arguments:
- pair: bfloat16 [896, 224, 128], P(('sample', 'row'), 'col'), parts along dimension 0, may hold values from -6 to 6
- pair_gain: float32 [128], replicated, may hold values from 0.1 to 1.9
- bias_weight: bfloat16 [128, 16], replicated, may hold values from -0.5 to 0.5
- single: bfloat16 [896, 384], P(('sample', 'row', 'col')), parts along dimension 0, may hold values from -50 to 50
- w_query: bfloat16 [384, 384], replicated, may hold values from -0.30618622 to 0.30618622
- w_key: bfloat16 [384, 384], replicated, may hold values from -0.30618622 to 0.30618622
- w_value: bfloat16 [384, 384], replicated, may hold values from -0.3125 to 0.3125
- w_out: bfloat16 [384, 384], replicated, may hold values from -0.3125 to 0.3125
- key_mask: int32 [896], P(('sample', 'col')), parts along dimension 0, may hold values from 0 to 1, as said below
- out_grad: bfloat16 [896, 384], P(('sample', 'row', 'col')), parts along dimension 0, may hold values from -6 to 6
Outputs:
- pair_grad: bfloat16 [896, 224, 128], P(('sample', 'row'), 'col'), parts along dimension 0
- single_grad: bfloat16 [896, 384], P(('sample', 'row', 'col')), parts along dimension 0
- query_weight_grad: float32 [1536, 384], P(('sample', 'row', 'col')), parts along dimension 0
- key_weight_grad: float32 [1536, 384], P(('sample', 'row', 'col')), parts along dimension 0
- value_weight_grad: float32 [1536, 384], P(('sample', 'row', 'col')), parts along dimension 0
- out_weight_grad: float32 [1536, 384], P(('sample', 'row', 'col')), parts along dimension 0
- bias_weight_grad: float32 [512, 16], P('sample'), parts along dimension 0
- gain_grad: float32 [512], P('sample'), parts along dimension 0
The draws below stay inside these ranges and needn't reach their ends.
There are 4 independent parts, one for each index of `sample`. The reference program is written for one: setup_inputs(seed, part) draws one part's arguments, and reference() takes and returns one part's arrays. A program takes and returns all parts, laid end to end along the dimension named above; an argument that names none is the same for every part. Nothing has to cross between parts.
Inputs may be any that keep to these rules, and one draw needn't show every extreme that they name: key_mask is 1 exactly on a prefix of the tokens whose length is a multiple of 4, at least half of 224 and at most 220, and 0 after it.
All inputs are finite; a program needn't handle non-finite values.
Results may differ from the reference program's by a relative error of at most 0.04.
Values may be sent and summed in bfloat16 or wider, within the bound.
A program may use at most 64 MiB of HBM per device.

```python
import jax
import jax.numpy as jnp
from jax import lax

D = 384
PAIR = 128
HEADS = 16
HEAD = 24
PADBLOCK = 4
TOKENS = 224


def projection_pair(key):
    first_key = jax.random.fold_in(key, 7101)
    second_key = jax.random.fold_in(key, 7102)
    spread = D ** (-0.5)
    query_weight = jnp.clip(jax.random.normal(first_key, (D, D), jnp.float32), -6.0, 6.0) * spread
    noise_weight = jnp.clip(jax.random.normal(second_key, (D, D), jnp.float32), -6.0, 6.0) * spread
    key_weight = noise_weight
    return (query_weight, key_weight)


def draw_w_query(key, part):
    return projection_pair(key)[0].astype(jnp.bfloat16)


def draw_w_key(key, part):
    return projection_pair(key)[1].astype(jnp.bfloat16)


def draw_single(key, part):
    base = jnp.clip(jax.random.normal(jax.random.fold_in(key, 7201), (TOKENS, D), jnp.float32), -6.0, 6.0)
    return base.astype(jnp.bfloat16)


def draw_key_mask(key, part):
    block_count = TOKENS // PADBLOCK
    lowest = (block_count + 1) // 2
    highest_count = block_count - 1
    choices_count = highest_count - lowest + 1
    offset = jax.random.randint(jax.random.fold_in(key, 7301), (), 0, choices_count)
    part_index = jnp.asarray(part).astype(jnp.int32)
    blocks = lowest + (offset.astype(jnp.int32) + part_index) % choices_count
    live_count = blocks * PADBLOCK
    return (jnp.arange(TOKENS, dtype=jnp.int32) < live_count).astype(jnp.int32)


def levels(key, extent, pieces, smallest, high):
    factor_of = 1.0
    for dim, blocks in pieces:
        draws = jax.random.uniform(jax.random.fold_in(jax.random.fold_in(key, 6), dim), (blocks,), jnp.float32, smallest / len(pieces), high / len(pieces))
        factor_of = factor_of * jnp.repeat(jnp.exp(draws), extent[dim] // blocks).reshape((-1,) + (1,) * (len(extent) - 1 - dim))
    return factor_of


def scatter_about(key, extent, scale, most, pieces=(), kind=jnp.bfloat16):
    values = jax.random.normal(key, extent, jnp.float32) * scale
    if len(pieces) > 0:
        values = levels(key, extent, pieces, -0.22, 0.18) * values
    return jnp.clip(values, min=-most, max=most).astype(kind)


def setup_inputs(seed: int = 0, part: int = 0) -> dict:
    key_list = jax.random.split(jax.random.key(seed), 11)
    part_keys = jax.random.split(jax.random.fold_in(key_list[10], part), 11)
    pair = scatter_about(part_keys[0], (TOKENS, TOKENS, PAIR), 1.0, 6.0, ((0, 2), (1, 4)))
    pair_gain = jnp.clip(1.0 + 0.18 * jax.random.normal(key_list[1], (PAIR,), jnp.float32), 0.1, 1.9)
    bias_weight = scatter_about(key_list[2], (PAIR, HEADS), PAIR ** -0.5, 0.5)
    single = draw_single(jax.random.fold_in(jax.random.fold_in(key_list[10], part), 71), part)
    w_query = draw_w_query(jax.random.fold_in(key_list[10], 71), part)
    w_key = draw_w_key(jax.random.fold_in(key_list[10], 71), part)
    w_value = scatter_about(key_list[6], (D, D), D ** -0.5, 0.3125)
    w_out = scatter_about(key_list[7], (D, D), D ** -0.5, 0.3125)
    key_mask = draw_key_mask(jax.random.fold_in(jax.random.fold_in(key_list[10], part), 71), part)
    out_grad = scatter_about(part_keys[9], (TOKENS, D), 1.0, 6.0, ((0, 8),))
    return dict(pair=pair, pair_gain=pair_gain, bias_weight=bias_weight, single=single, w_query=w_query, w_key=w_key, w_value=w_value, w_out=w_out, key_mask=key_mask, out_grad=out_grad)


norm_eps = 1e-05
masked_score = -1000000000.0
highest = lax.Precision.HIGHEST

def project(grads, weight):
    return jnp.dot(grads, weight.astype(jnp.float32).T, precision=highest)

def transposed_product(left, right):
    return jnp.dot(left.astype(jnp.float32).T, right, precision=highest)

def reference(pair, pair_gain, bias_weight, single, w_query, w_key, w_value, w_out, key_mask, out_grad):
    f32 = jnp.float32
    bf16 = jnp.bfloat16
    tokens = single.shape[0]
    width = single.shape[1]
    score_scale = HEAD ** (-0.5)
    pair_float = pair.astype(f32)
    centred = pair_float - lax.optimization_barrier(jnp.mean(pair_float, axis=2, keepdims=True))
    inverse = lax.rsqrt(lax.optimization_barrier(jnp.mean(centred * centred, axis=2, keepdims=True)) + norm_eps)
    normed = centred * inverse
    pair_normed = (normed * pair_gain).astype(bf16)
    pair_bias = jnp.einsum('ijc,ch->hij', pair_normed.astype(f32), bias_weight.astype(f32))
    query = jnp.dot(single, w_query, preferred_element_type=f32).astype(bf16)
    key = jnp.dot(single, w_key, preferred_element_type=f32).astype(bf16)
    value = jnp.dot(single, w_value, preferred_element_type=f32).astype(bf16)
    query_heads = query.astype(f32).reshape(tokens, HEADS, HEAD)
    key_heads = key.astype(f32).reshape(tokens, HEADS, HEAD)
    value_heads = value.astype(f32).reshape(tokens, HEADS, HEAD)
    scores = jnp.einsum('ihd,jhd->hij', query_heads, key_heads) * score_scale + pair_bias
    scores = jnp.where(key_mask[None, None, :] > 0, scores, masked_score)
    row_top = lax.optimization_barrier(jnp.max(scores, axis=2, keepdims=True))
    exp_scores = jnp.exp(scores - row_top)
    probs = exp_scores / lax.optimization_barrier(jnp.sum(exp_scores, axis=2, keepdims=True))
    probs_low = probs.astype(bf16)
    attended = jnp.einsum('hij,jhd->ihd', probs_low.astype(f32), value_heads)
    attended_flat = attended.reshape(tokens, width)
    attended_low = attended_flat.astype(bf16)
    grad_att = jnp.dot(out_grad, w_out.T, preferred_element_type=f32).astype(bf16)
    grad_heads = grad_att.astype(f32).reshape(tokens, HEADS, HEAD)
    grad_probs = jnp.einsum('ihd,jhd->hij', grad_heads, value_heads)
    row_delta = jnp.einsum('ihd,ihd->hi', grad_heads, attended)
    grad_scores = probs * (grad_probs - row_delta[:, :, None])
    grad_low = grad_scores.astype(bf16).astype(f32)
    query_grad = (jnp.einsum('hij,jhd->ihd', grad_low, key_heads) * score_scale).reshape(tokens, width)
    key_grad = (jnp.einsum('hij,ihd->jhd', grad_low, query_heads) * score_scale).reshape(tokens, width)
    value_grad = jnp.einsum('hij,ihd->jhd', probs_low.astype(f32), grad_heads).reshape(tokens, width)
    single_grad = (project(query_grad, w_query) + project(key_grad, w_key) + project(value_grad, w_value)).astype(bf16)
    query_weight_grad = transposed_product(single, query_grad)
    key_weight_grad = transposed_product(single, key_grad)
    value_weight_grad = transposed_product(single, value_grad)
    out_weight_grad = jnp.dot(attended_low.T, out_grad, preferred_element_type=f32)
    grad_normed = jnp.einsum('hij,ch->ijc', grad_low, bias_weight.astype(f32))
    bias_weight_grad = jnp.einsum('ijc,hij->ch', pair_normed.astype(f32), grad_low)
    gain_grad = lax.optimization_barrier(jnp.sum(grad_normed * normed, axis=(0, 1)))
    scaled = grad_normed * pair_gain
    pair_grad = (inverse * (scaled - lax.optimization_barrier(jnp.mean(scaled, axis=2, keepdims=True)) - normed * lax.optimization_barrier(jnp.mean(scaled * normed, axis=2, keepdims=True)))).astype(bf16)
    return (pair_grad, single_grad, query_weight_grad, key_weight_grad, value_weight_grad, out_weight_grad, bias_weight_grad, gain_grad)
```

```python
import functools

import jax
import jax.numpy as jnp
from jax import lax
from jax.experimental import pallas as pl
from jax.experimental.pallas import tpu as pltpu
from jax.sharding import PartitionSpec as P

HEADS = 16
HEAD = 24

norm_eps = 1e-05
masked_score = -1000000000.0
f32 = jnp.float32
bf16 = jnp.bfloat16
MESH = pl.DeviceIdType.MESH


def dot(a, b, contract=((1,), (0,))):
    return lax.dot_general(a, b, (contract, ((), ())), preferred_element_type=f32)


def dot_nt(a, b):
    return dot(a, b, ((1,), (1,)))


def dot_tn(a, b):
    return dot(a, b, ((0,), (0,)))


def iota(shape, dim):
    return lax.broadcasted_iota(jnp.int32, shape, dim).astype(f32)


def whole(x, unit):
    return jnp.floor((x + 0.5) * (1.0 / unit))


def one_hot(condition):
    return jnp.where(condition, 1.0, 0.0).astype(bf16)


def each(first, last, step):
    if last - first <= 16:
        for k in range(first, last):
            step(k)
    else:
        pl.loop(first, last)(step)


def kernel(
    rows,
    cols,
    pair,
    gain_ref,
    bw,
    single,
    wq,
    wk,
    wv,
    wo,
    mask_ref,
    og,
    pair_grad,
    single_grad,
    wgq,
    wgk,
    wgv,
    wgo,
    bwg,
    gg,
    sbuf,
    gbuf,
    stat,
    a_send,
    a_recv,
    q_send,
    q_recv,
    kv_send,
    kv_recv,
    ag,
    fin,
    normed,
    inv,
    ebuf,
    gpbuf,
    plow,
    glow,
    qd,
    gd,
    hm,
    stat_rows,
    att_acc,
    qg_acc,
    kg_acc,
    vg_acc,
    bw_acc,
    gain_acc,
    sems,
    stat_sems,
    a_sems,
    q_sems,
    kv_sems,
):
    group = rows * cols
    own, width = single.shape
    padded = sbuf.shape[1]
    row_count, col_count, channels = pair.shape
    row = lax.axis_index("row")
    col = lax.axis_index("col")
    me = row * cols + col
    scale = HEAD ** (-0.5)
    chunk = 16 if row_count % 16 == 0 else 8 if row_count % 8 == 0 else row_count
    crows = chunk * HEADS
    pad_rows = cols * padded
    pad_cols = rows * padded

    def device(index):
        return {"row": index // cols, "col": index % cols}

    def peer(k):
        return lax.rem(me + k, group)

    def sender(k):
        return lax.rem(me + group - k, group)

    barrier = pltpu.get_barrier_semaphore()

    def greet(k):
        pl.semaphore_signal(barrier, inc=1, device_id=device(peer(k)), device_id_type=MESH)

    each(1, group, greet)

    def gather(buf, kind):
        def copy(k, slot):
            return pltpu.make_async_remote_copy(
                src_ref=buf.at[me],
                dst_ref=buf.at[slot],
                send_sem=sems.at[2 * kind, k],
                recv_sem=sems.at[2 * kind + 1, k],
                device_id=device(peer(k)),
                device_id_type=MESH,
            )

        return (
            lambda: each(1, group, lambda k: copy(k, me).start()),
            lambda: each(1, group, lambda k: copy(k, sender(k)).wait_recv()),
            lambda: each(1, group, lambda k: copy(k, me).wait_send()),
        )

    def along_col(src_of, buf, col_sems):
        def copy(k, slot):
            target = lax.rem(col + k, cols)
            return pltpu.make_async_remote_copy(
                src_ref=src_of(target),
                dst_ref=buf.at[slot],
                send_sem=col_sems.at[0, k],
                recv_sem=col_sems.at[1, k],
                device_id={"row": row, "col": target},
                device_id_type=MESH,
            )

        return (
            lambda: each(1, cols, lambda k: copy(k, col).start()),
            lambda: each(
                1, cols, lambda k: copy(k, lax.rem(col + cols - k, cols)).wait_recv()
            ),
            lambda: each(1, cols, lambda k: copy(k, col).wait_send()),
        )

    s_start, s_recv, s_sent = gather(sbuf, 0)
    g_start, g_recv, g_sent = gather(gbuf, 1)
    ag_start, ag_recv, ag_sent = gather(ag, 2)
    fin_start, fin_recv, fin_sent = gather(fin, 3)
    st_start, st_recv, st_sent = along_col(lambda target: stat.at[col], stat, stat_sems)
    a_start, a_wait, a_sent = along_col(lambda target: a_send.at[target], a_recv, a_sems)
    q_start, q_wait, q_sent = along_col(lambda target: q_send.at[target], q_recv, q_sems)

    pad_own = one_hot(iota((padded, own), 0) == iota((padded, own), 1))
    sbuf[me] = dot(pad_own, single[...]).astype(bf16)
    gbuf[me] = dot(pad_own, og[...]).astype(bf16)
    pl.semaphore_wait(barrier, group - 1)
    s_start()
    g_start()

    gain = gain_ref[...]
    eye = one_hot(iota((HEADS, HEADS), 0) == iota((HEADS, HEADS), 1))
    bw_t = dot_nt(eye, bw[...]).astype(bf16)

    def forward_row(i):
        x = pair[i].astype(f32)
        centred = x - jnp.mean(x, axis=1, keepdims=True)
        inverse = lax.rsqrt(jnp.mean(centred * centred, axis=1, keepdims=True) + norm_eps)
        norm = centred * inverse
        normed[i] = norm
        inv[i] = inverse
        ebuf[pl.ds(pl.multiple_of(i * HEADS, HEADS), HEADS), :] = dot_nt(
            bw_t, (norm * gain).astype(bf16)
        )

    unroll = 8 if row_count % 8 == 0 else 1

    @pl.loop(0, row_count // unroll)
    def _(block):
        for u in range(unroll):
            forward_row(block * unroll + u)

    line = iota((crows, 1), 0)
    line_query = whole(line, HEADS)
    line_head = line - line_query * HEADS
    hm[...] = jnp.where(whole(iota((1, width), 1), HEAD) == line_head, 1.0, 0.0)
    lane_gap = iota((1, 128), 1) - line_head
    slot_of = iota((1, pad_rows), 1)
    slot_in = slot_of - whole(slot_of, padded) * padded
    slot_token = jnp.where(slot_in < own, whole(slot_of, padded) * own + slot_in, -1.0)
    slot_of_t = iota((pad_rows, 1), 0)
    slot_in_t = slot_of_t - whole(slot_of_t, padded) * padded
    slot_token_t = jnp.where(
        slot_in_t < own, whole(slot_of_t, padded) * own + slot_in_t, -1.0
    )
    line_query_t = whole(iota((1, crows), 1), HEADS)
    key_slot = iota((1, pad_cols), 1)
    key_in = key_slot - whole(key_slot, padded) * padded
    key_token = jnp.where(key_in < own, whole(key_slot, padded) * own + key_in, -1.0)
    key_slot_t = iota((pad_cols, 1), 0)
    key_in_t = key_slot_t - whole(key_slot_t, padded) * padded
    key_token_t = jnp.where(key_in_t < own, whole(key_slot_t, padded) * own + key_in_t, -1.0)
    pick_keys = one_hot(key_token == iota((col_count, 1), 0))
    pick_keys_t = one_hot(key_token_t == iota((1, col_count), 1))

    s_recv()
    row_tokens = sbuf[pl.ds(row * cols, cols)].reshape(pad_rows, width)
    col_tokens = sbuf[pl.ds(col * rows, rows)].reshape(pad_cols, width)
    query = dot(row_tokens, wq[...]).astype(bf16)
    key = dot(pick_keys, dot(col_tokens, wk[...]).astype(bf16)).astype(bf16)
    value = dot(pick_keys, dot(col_tokens, wv[...]).astype(bf16)).astype(bf16)
    g_recv()
    grad_tokens = gbuf[pl.ds(row * cols, cols)].reshape(pad_rows, width)
    grad_att = dot_nt(grad_tokens, wo[...]).astype(bf16)
    live = mask_ref[...] > 0

    @pl.loop(0, row_count // chunk)
    def _(block):
        lines = pl.ds(pl.multiple_of(block * crows, crows), crows)
        first = (block * chunk).astype(f32)
        spread = one_hot(slot_token == line_query + first)
        q_diag = (dot(spread, query) * hm[...]).astype(bf16)
        g_diag = (dot(spread, grad_att) * hm[...]).astype(bf16)
        qd[lines, :] = q_diag
        gd[lines, :] = g_diag
        scores = dot_nt(q_diag, key) * scale + ebuf[lines, :]
        scores = jnp.where(live, scores, masked_score)
        top = jnp.max(scores, axis=1, keepdims=True)
        exps = jnp.exp(scores - top)
        grad_probs = dot_nt(g_diag, value)
        total = jnp.sum(exps, axis=1, keepdims=True)
        part = jnp.sum(exps * grad_probs, axis=1, keepdims=True)
        ebuf[lines, :] = exps
        gpbuf[lines, :] = grad_probs
        placed = jnp.where(
            lane_gap == 0.0,
            top,
            jnp.where(
                lane_gap == float(HEADS), total, jnp.where(lane_gap == 2.0 * HEADS, part, 0.0)
            ),
        )
        stat_rows[pl.ds(pl.multiple_of(block * chunk, chunk), chunk), :] = jnp.sum(
            placed.reshape(chunk, HEADS, 128), axis=1
        )

    stat[col] = stat_rows[...].T[: 3 * HEADS]
    st_start()
    st_recv()
    own_top = stat[col, 0:HEADS]
    row_top = stat[0, 0:HEADS]
    for k in range(1, cols):
        row_top = jnp.maximum(row_top, stat[k, 0:HEADS])
    row_total = jnp.zeros_like(row_top)
    delta = jnp.zeros_like(row_top)
    for k in range(cols):
        weight = jnp.exp(stat[k, 0:HEADS] - row_top)
        row_total += weight * stat[k, HEADS : 2 * HEADS]
        delta += weight * stat[k, 2 * HEADS : 3 * HEADS]
    factor = jnp.exp(own_top - row_top) / row_total
    delta = delta / row_total
    stat_rows[...] = jnp.concatenate(
        [factor, delta, jnp.zeros((128 - 2 * HEADS, row_count), f32)], axis=0
    ).T

    att_acc[...] = jnp.zeros_like(att_acc)
    qg_acc[...] = jnp.zeros_like(qg_acc)
    kg_acc[...] = jnp.zeros_like(kg_acc)
    vg_acc[...] = jnp.zeros_like(vg_acc)

    @pl.loop(0, row_count // chunk)
    def _(block):
        lines = pl.ds(pl.multiple_of(block * crows, crows), crows)
        first = (block * chunk).astype(f32)
        stats = stat_rows[pl.ds(pl.multiple_of(block * chunk, chunk), chunk), :]
        stats = jnp.broadcast_to(stats[:, None, :], (chunk, HEADS, 128)).reshape(crows, 128)
        factor = jnp.sum(jnp.where(lane_gap == 0.0, stats, 0.0), axis=1, keepdims=True)
        delta = jnp.sum(jnp.where(lane_gap == float(HEADS), stats, 0.0), axis=1, keepdims=True)
        probs = ebuf[lines, :] * factor
        probs_low = probs.astype(bf16)
        grad_low = (probs * (gpbuf[lines, :] - delta)).astype(bf16)
        glow[lines, :] = grad_low
        fold = one_hot(slot_token_t == line_query_t + first)
        att = (dot(probs_low, value) * hm[...]).astype(bf16)
        att_acc[...] += dot(fold, att)
        query_grad = (dot(grad_low, key) * (scale * hm[...])).astype(bf16)
        qg_acc[...] += dot(fold, query_grad)
        kg_acc[...] += dot_tn(grad_low, qd[lines, :])
        vg_acc[...] += dot_tn(probs_low, gd[lines, :])

    a_send[...] = att_acc[...].reshape(cols, padded, width).astype(bf16)
    q_send[...] = qg_acc[...].reshape(cols, padded, width).astype(bf16)
    key_side = dot(pick_keys_t, (kg_acc[...] * scale).astype(bf16))
    value_side = dot(pick_keys_t, vg_acc[...].astype(bf16))
    kv_send[:, 0] = key_side.reshape(rows, padded, width).astype(bf16)
    kv_send[:, 1] = value_side.reshape(rows, padded, width).astype(bf16)

    def kv_copy(b, slot):
        return pltpu.make_async_remote_copy(
            src_ref=kv_send.at[b],
            dst_ref=kv_recv.at[slot],
            send_sem=kv_sems.at[0, b],
            recv_sem=kv_sems.at[1, slot],
            device_id=device(col * rows + b),
            device_id_type=MESH,
        )

    def kv_start(b):
        pl.when(col * rows + b != me)(lambda: kv_copy(b, row).start())

    def kv_sent(b):
        pl.when(col * rows + b != me)(lambda: kv_copy(b, row).wait_send())

    def kv_wait(r):
        pl.when(r * cols + me // rows != me)(lambda: kv_copy(0, r).wait_recv())

    each(0, rows, kv_start)
    q_start()
    a_start()
    a_recv[col] = a_send[col]
    q_recv[col] = q_send[col]

    @pl.when(me // rows == col)
    def _():
        kv_recv[row] = kv_send[me % rows]

    bw_acc[...] = jnp.zeros_like(bw_acc)
    gain_acc[...] = jnp.zeros_like(gain_acc)

    def backward_row(i):
        grad_low = glow[pl.ds(pl.multiple_of(i * HEADS, HEADS), HEADS), :]
        norm = normed[i]
        grad_normed = dot_tn(grad_low, bw_t)
        bw_part = dot(grad_low, (norm * gain).astype(bf16))
        scaled = grad_normed * gain
        gain_part = grad_normed * norm
        along = jnp.mean(gain_part * gain, axis=1, keepdims=True)
        pair_grad[i] = (
            inv[i] * (scaled - jnp.mean(scaled, axis=1, keepdims=True) - norm * along)
        ).astype(bf16)
        return bw_part, gain_part

    def backward(first, last):
        @pl.loop(first // unroll, last // unroll)
        def _(block):
            bw_sum = bw_acc[...]
            gain_sum = gain_acc[...]
            for u in range(unroll):
                bw_part, gain_part = backward_row(block * unroll + u)
                bw_sum += bw_part
                gain_sum += gain_part
            bw_acc[...] = bw_sum
            gain_acc[...] = gain_sum

    split = (row_count // unroll // 2) * unroll
    backward(0, split)

    a_wait()
    q_wait()
    each(0, rows, kv_wait)
    att_own = a_recv[0].astype(f32)
    qg_own = q_recv[0].astype(f32)
    for k in range(1, cols):
        att_own += a_recv[k].astype(f32)
        qg_own += q_recv[k].astype(f32)
    kg_own = kv_recv[0, 0].astype(f32)
    vg_own = kv_recv[0, 1].astype(f32)
    for k in range(1, rows):
        kg_own += kv_recv[k, 0].astype(f32)
        vg_own += kv_recv[k, 1].astype(f32)
    qg_low = qg_own.astype(bf16)
    kg_low = kg_own.astype(bf16)
    vg_low = vg_own.astype(bf16)
    ag[me, 0] = qg_low
    ag[me, 1] = kg_low
    ag[me, 2] = vg_low
    ag[me, 3] = att_own.astype(bf16)
    ag_start()

    backward(split, row_count)
    fin[me, 0:HEADS] = bw_acc[...]
    fin[me, HEADS : HEADS + 8] = jnp.broadcast_to(
        jnp.sum(gain_acc[...], axis=0, keepdims=True), (8, channels)
    )
    fin_start()
    out_rows = dot_nt(qg_low, wq[...]) + dot_nt(kg_low, wk[...]) + dot_nt(vg_low, wv[...])
    single_grad[...] = out_rows[:own].astype(bf16)

    share = wgq.shape[0]
    share_pad = (share + 15) // 16 * 16
    pick = one_hot(
        iota((share_pad, width), 1)
        == iota((share_pad, width), 0) + (me * share).astype(f32)
    )
    tokens_t = dot_nt(pick, sbuf[...].reshape(group * padded, width)).astype(bf16)
    ag_recv()
    for k, out in enumerate((wgq, wgk, wgv)):
        out[...] = dot(tokens_t, ag[:, k].reshape(group * padded, width))[:share]
    att_t = dot_nt(pick, ag[:, 3].reshape(group * padded, width)).astype(bf16)
    wgo[...] = dot(att_t, gbuf[...].reshape(group * padded, width))[:share]

    fin_recv()
    total_parts = fin[0]
    for k in range(1, group):
        total_parts += fin[k]
    bwg[...] = total_parts[0:HEADS].T
    gg[...] = total_parts[HEADS : HEADS + 1]
    s_sent()
    g_sent()
    st_sent()
    a_sent()
    q_sent()
    each(0, rows, kv_sent)
    ag_sent()
    fin_sent()


def body(rows, cols, pair, pair_gain, bias_weight, single, w_query, w_key, w_value, w_out, key_mask, out_grad):
    row_count, col_count, channels = pair.shape
    own, width = single.shape
    group = rows * cols
    padded = (own + 15) // 16 * 16
    lines = row_count * HEADS
    share = width // group
    chunk = 16 if row_count % 16 == 0 else 8 if row_count % 8 == 0 else row_count
    vmem = pl.BlockSpec(memory_space=pltpu.VMEM)
    shape = jax.ShapeDtypeStruct
    outs = pl.pallas_call(
        functools.partial(kernel, rows, cols),
        out_shape=(
            shape(pair.shape, bf16),
            shape(single.shape, bf16),
            shape((share, width), f32),
            shape((share, width), f32),
            shape((share, width), f32),
            shape((share, width), f32),
            shape((channels, HEADS), f32),
            shape((1, channels), f32),
        ),
        in_specs=[vmem] * 10,
        out_specs=(vmem,) * 8,
        scratch_shapes=[
            pltpu.VMEM((group, padded, width), bf16),
            pltpu.VMEM((group, padded, width), bf16),
            pltpu.VMEM((cols, 3 * HEADS, row_count), f32),
            pltpu.VMEM((cols, padded, width), bf16),
            pltpu.VMEM((cols, padded, width), bf16),
            pltpu.VMEM((cols, padded, width), bf16),
            pltpu.VMEM((cols, padded, width), bf16),
            pltpu.VMEM((rows, 2, padded, width), bf16),
            pltpu.VMEM((rows, 2, padded, width), bf16),
            pltpu.VMEM((group, 4, padded, width), bf16),
            pltpu.VMEM((group, HEADS + 8, channels), f32),
            pltpu.VMEM((row_count, col_count, channels), f32),
            pltpu.VMEM((row_count, col_count, 1), f32),
            pltpu.VMEM((lines, col_count), f32),
            pltpu.VMEM((lines, col_count), f32),
            pltpu.VMEM((16, 128), bf16),
            pltpu.VMEM((lines, col_count), bf16),
            pltpu.VMEM((lines, width), bf16),
            pltpu.VMEM((lines, width), bf16),
            pltpu.VMEM((chunk * HEADS, width), f32),
            pltpu.VMEM((row_count, 128), f32),
            pltpu.VMEM((cols * padded, width), f32),
            pltpu.VMEM((cols * padded, width), f32),
            pltpu.VMEM((col_count, width), f32),
            pltpu.VMEM((col_count, width), f32),
            pltpu.VMEM((HEADS, channels), f32),
            pltpu.VMEM((col_count, channels), f32),
            pltpu.SemaphoreType.DMA((8, group)),
            pltpu.SemaphoreType.DMA((2, cols)),
            pltpu.SemaphoreType.DMA((2, cols)),
            pltpu.SemaphoreType.DMA((2, cols)),
            pltpu.SemaphoreType.DMA((2, rows)),
        ],
        compiler_params=pltpu.CompilerParams(
            collective_id=0, has_side_effects=True, vmem_limit_bytes=50 * 1024 * 1024
        ),
    )(
        pair,
        pair_gain.reshape(1, channels),
        bias_weight,
        single,
        w_query,
        w_key,
        w_value,
        w_out,
        key_mask.reshape(1, col_count),
        out_grad,
    )
    return outs[:-1] + (outs[-1].reshape(channels),)


def solution(mesh):
    tokens = ("sample", "row", "col")
    in_specs = (
        P(("sample", "row"), "col", None),
        P(),
        P(),
        P(tokens, None),
        P(),
        P(),
        P(),
        P(),
        P(("sample", "col")),
        P(tokens, None),
    )
    out_specs = (
        P(("sample", "row"), "col", None),
        P(tokens, None),
        P(tokens, None),
        P(tokens, None),
        P(tokens, None),
        P(tokens, None),
        P("sample", None),
        P("sample"),
    )
    return jax.shard_map(
        functools.partial(body, mesh.shape["row"], mesh.shape["col"]),
        mesh=mesh,
        in_specs=in_specs,
        out_specs=out_specs,
        check_vma=False,
    )
```

```python
import functools

import jax
import jax.numpy as jnp
from jax import lax
from jax.experimental import pallas as pl
from jax.experimental.pallas import tpu as pltpu
from jax.sharding import PartitionSpec as P

HEADS = 16
HEAD = 24

norm_eps = 1e-05
masked_score = -1000000000.0
f32 = jnp.float32
bf16 = jnp.bfloat16
MESH = pl.DeviceIdType.MESH


def dot(a, b, contract=((1,), (0,))):
    return lax.dot_general(a, b, (contract, ((), ())), preferred_element_type=f32)


def dot_nt(a, b):
    return dot(a, b, ((1,), (1,)))


def dot_tn(a, b):
    return dot(a, b, ((0,), (0,)))


def iota(shape, dim):
    return lax.broadcasted_iota(jnp.int32, shape, dim).astype(f32)


def whole(x, unit):
    return jnp.floor((x + 0.5) * (1.0 / unit))


def one_hot(condition):
    return jnp.where(condition, 1.0, 0.0).astype(bf16)


def each(first, last, step):
    if last - first <= 16:
        for k in range(first, last):
            step(k)
    else:
        pl.loop(first, last)(step)


def kernel(
    rows,
    cols,
    pair_hbm,
    gain_hbm,
    bw_hbm,
    single_hbm,
    wq_hbm,
    wk_hbm,
    wv_hbm,
    wo_hbm,
    mask_hbm,
    og_hbm,
    pair_grad,
    single_grad,
    wgq,
    wgk,
    wgv,
    wgo,
    bwg,
    gg,
    sbuf,
    gbuf,
    stat,
    a_send,
    a_recv,
    q_send,
    q_recv,
    kv_send,
    kv_recv,
    ag,
    fin,
    normed,
    inv,
    ebuf,
    gpbuf,
    plow,
    glow,
    qd,
    gd,
    hm,
    stat_rows,
    att_acc,
    qg_acc,
    kg_acc,
    vg_acc,
    bw_acc,
    gain_acc,
    sems,
    stat_sems,
    a_sems,
    q_sems,
    kv_sems,
    s_sems,
    g_sems,
    ag_sems,
    s_row_sems,
    g_row_sems,
    ag_row_sems,
    pair,
    gain_ref,
    bw,
    single,
    wq,
    wk,
    wv,
    wo,
    mask_ref,
    og,
    in_sems,
):
    group = rows * cols
    own, width = single.shape
    padded = sbuf.shape[1]
    row_count, col_count, channels = pair.shape
    row = lax.axis_index("row")
    col = lax.axis_index("col")
    me = row * cols + col
    scale = HEAD ** (-0.5)
    chunk = 16 if row_count % 16 == 0 else 8 if row_count % 8 == 0 else row_count
    crows = chunk * HEADS
    pad_rows = cols * padded
    pad_cols = rows * padded

    def device(index):
        return {"row": index // cols, "col": index % cols}

    def peer(k):
        return lax.rem(me + k, group)

    def sender(k):
        return lax.rem(me + group - k, group)

    loads = [
        pltpu.make_async_copy(source, target, in_sems.at[k])
        for k, (source, target) in enumerate(
            (
                (single_hbm, single),
                (og_hbm, og),
                (gain_hbm, gain_ref),
                (bw_hbm, bw),
                (pair_hbm, pair),
                (wq_hbm, wq),
                (wk_hbm, wk),
                (wv_hbm, wv),
                (wo_hbm, wo),
                (mask_hbm, mask_ref),
            )
        )
    ]
    barrier = pltpu.get_barrier_semaphore()

    def greet(k):
        pl.semaphore_signal(barrier, inc=1, device_id=device(peer(k)), device_id_type=MESH)

    each(1, group, greet)
    for load in loads:
        load.start()

    def gather(buf, kind):
        def direct(k, slot):
            return pltpu.make_async_remote_copy(
                src_ref=buf.at[me],
                dst_ref=buf.at[slot],
                send_sem=sems.at[2 * kind, k],
                recv_sem=sems.at[2 * kind + 1, k],
                device_id=device(peer(k)),
                device_id_type=MESH,
            )

        return (
            lambda: each(1, group, lambda k: direct(k, me).start()),
            lambda: each(1, group, lambda k: direct(k, sender(k)).wait_recv()),
            lambda: each(1, group, lambda k: direct(k, me).wait_send()),
        )

    def gather_two(buf, col_sems, row_sems):
        def across(k, slot):
            return pltpu.make_async_remote_copy(
                src_ref=buf.at[me],
                dst_ref=buf.at[slot],
                send_sem=col_sems.at[0, k],
                recv_sem=col_sems.at[1, k],
                device_id={"row": row, "col": lax.rem(col + k, cols)},
                device_id_type=MESH,
            )

        def relay(j, k, slot_row):
            place = lax.rem(col + cols - k, cols)
            return pltpu.make_async_remote_copy(
                src_ref=buf.at[row * cols + place],
                dst_ref=buf.at[slot_row * cols + place],
                send_sem=row_sems.at[0, j, k],
                recv_sem=row_sems.at[1, j, k],
                device_id={"row": lax.rem(row + j, rows), "col": col},
                device_id_type=MESH,
            )

        def start():
            each(1, cols, lambda k: across(k, me).start())
            each(1, rows, lambda j: relay(j, 0, row).start())

        def pass_on():
            def one(k):
                across(k, row * cols + lax.rem(col + cols - k, cols)).wait_recv()
                each(1, rows, lambda j: relay(j, k, row).start())

            each(1, cols, one)

        def receive():
            def one(j):
                slot_row = lax.rem(row + rows - j, rows)
                each(0, cols, lambda k: relay(j, k, slot_row).wait_recv())

            each(1, rows, one)

        def sent():
            each(1, cols, lambda k: across(k, me).wait_send())
            each(1, rows, lambda j: each(0, cols, lambda k: relay(j, k, row).wait_send()))

        return start, pass_on, receive, sent

    def along_col(src_of, buf, col_sems):
        def copy(k, slot):
            target = lax.rem(col + k, cols)
            return pltpu.make_async_remote_copy(
                src_ref=src_of(target),
                dst_ref=buf.at[slot],
                send_sem=col_sems.at[0, k],
                recv_sem=col_sems.at[1, k],
                device_id={"row": row, "col": target},
                device_id_type=MESH,
            )

        return (
            lambda: each(1, cols, lambda k: copy(k, col).start()),
            lambda: each(
                1, cols, lambda k: copy(k, lax.rem(col + cols - k, cols)).wait_recv()
            ),
            lambda: each(1, cols, lambda k: copy(k, col).wait_send()),
        )

    s_start, s_pass, s_recv, s_sent = gather_two(sbuf, s_sems, s_row_sems)
    g_start, g_pass, g_recv, g_sent = gather_two(gbuf, g_sems, g_row_sems)
    ag_start, ag_pass, ag_recv, ag_sent = gather_two(ag, ag_sems, ag_row_sems)
    fin_start, fin_recv, fin_sent = gather(fin, 0)
    st_start, st_recv, st_sent = along_col(lambda target: stat.at[col], stat, stat_sems)
    a_start, a_wait, a_sent = along_col(lambda target: a_send.at[target], a_recv, a_sems)
    q_start, q_wait, q_sent = along_col(lambda target: q_send.at[target], q_recv, q_sems)

    loads[0].wait()
    loads[1].wait()
    pad_own = one_hot(iota((padded, own), 0) == iota((padded, own), 1))
    sbuf[me] = dot(pad_own, single[...]).astype(bf16)
    gbuf[me] = dot(pad_own, og[...]).astype(bf16)
    pl.semaphore_wait(barrier, group - 1)
    s_start()
    g_start()

    for load in loads[2:5]:
        load.wait()
    gain = gain_ref[...]
    bw_t = bw[...]

    def forward_row(i):
        x = pair[i].astype(f32)
        centred = x - jnp.mean(x, axis=1, keepdims=True)
        inverse = lax.rsqrt(jnp.mean(centred * centred, axis=1, keepdims=True) + norm_eps)
        norm = centred * inverse
        normed[i] = norm
        inv[i] = inverse
        ebuf[pl.ds(pl.multiple_of(i * HEADS, HEADS), HEADS), :] = dot_nt(
            bw_t, (norm * gain).astype(bf16)
        )

    unroll = 8 if row_count % 8 == 0 else 1

    @pl.loop(0, row_count // unroll)
    def _(block):
        for u in range(unroll):
            forward_row(block * unroll + u)

    line = iota((crows, 1), 0)
    line_query = whole(line, HEADS)
    line_head = line - line_query * HEADS
    hm[...] = jnp.where(whole(iota((1, width), 1), HEAD) == line_head, 1.0, 0.0)
    lane_gap = iota((1, 128), 1) - line_head
    slot_of = iota((1, pad_rows), 1)
    slot_in = slot_of - whole(slot_of, padded) * padded
    slot_token = jnp.where(slot_in < own, whole(slot_of, padded) * own + slot_in, -1.0)
    slot_of_t = iota((pad_rows, 1), 0)
    slot_in_t = slot_of_t - whole(slot_of_t, padded) * padded
    slot_token_t = jnp.where(
        slot_in_t < own, whole(slot_of_t, padded) * own + slot_in_t, -1.0
    )
    line_query_t = whole(iota((1, crows), 1), HEADS)
    key_slot = iota((1, pad_cols), 1)
    key_in = key_slot - whole(key_slot, padded) * padded
    key_token = jnp.where(key_in < own, whole(key_slot, padded) * own + key_in, -1.0)
    key_slot_t = iota((pad_cols, 1), 0)
    key_in_t = key_slot_t - whole(key_slot_t, padded) * padded
    key_token_t = jnp.where(key_in_t < own, whole(key_slot_t, padded) * own + key_in_t, -1.0)
    pick_keys = one_hot(key_token == iota((col_count, 1), 0))
    pick_keys_t = one_hot(key_token_t == iota((1, col_count), 1))

    for load in loads[5:]:
        load.wait()
    s_pass()
    s_recv()
    row_tokens = sbuf[pl.ds(row * cols, cols)].reshape(pad_rows, width)
    col_tokens = sbuf[pl.ds(col * rows, rows)].reshape(pad_cols, width)
    query = dot(row_tokens, wq[...]).astype(bf16)
    key = dot(pick_keys, dot(col_tokens, wk[...]).astype(bf16)).astype(bf16)
    value = dot(pick_keys, dot(col_tokens, wv[...]).astype(bf16)).astype(bf16)
    g_pass()
    grad_tokens = gbuf[pl.ds(row * cols, cols)].reshape(pad_rows, width)
    grad_att = dot_nt(grad_tokens, wo[...]).astype(bf16)
    live = mask_ref[...] > 0

    @pl.loop(0, row_count // chunk)
    def _(block):
        lines = pl.ds(pl.multiple_of(block * crows, crows), crows)
        first = (block * chunk).astype(f32)
        spread = one_hot(slot_token == line_query + first)
        q_diag = (dot(spread, query) * hm[...]).astype(bf16)
        g_diag = (dot(spread, grad_att) * hm[...]).astype(bf16)
        qd[lines, :] = q_diag
        gd[lines, :] = g_diag
        scores = dot_nt(q_diag, key) * scale + ebuf[lines, :]
        scores = jnp.where(live, scores, masked_score)
        top = jnp.max(scores, axis=1, keepdims=True)
        exps = jnp.exp(scores - top)
        grad_probs = dot_nt(g_diag, value)
        total = jnp.sum(exps, axis=1, keepdims=True)
        part = jnp.sum(exps * grad_probs, axis=1, keepdims=True)
        ebuf[lines, :] = exps
        gpbuf[lines, :] = grad_probs
        placed = jnp.where(
            lane_gap == 0.0,
            top,
            jnp.where(
                lane_gap == float(HEADS), total, jnp.where(lane_gap == 2.0 * HEADS, part, 0.0)
            ),
        )
        stat_rows[pl.ds(pl.multiple_of(block * chunk, chunk), chunk), :] = jnp.sum(
            placed.reshape(chunk, HEADS, 128), axis=1
        )

    stat[col] = stat_rows[...].T[: 3 * HEADS]
    st_start()
    st_recv()
    own_top = stat[col, 0:HEADS]
    row_top = stat[0, 0:HEADS]
    for k in range(1, cols):
        row_top = jnp.maximum(row_top, stat[k, 0:HEADS])
    row_total = jnp.zeros_like(row_top)
    delta = jnp.zeros_like(row_top)
    for k in range(cols):
        weight = jnp.exp(stat[k, 0:HEADS] - row_top)
        row_total += weight * stat[k, HEADS : 2 * HEADS]
        delta += weight * stat[k, 2 * HEADS : 3 * HEADS]
    factor = jnp.exp(own_top - row_top) / row_total
    delta = delta / row_total
    stat_rows[...] = jnp.concatenate(
        [factor, delta, jnp.zeros((128 - 2 * HEADS, row_count), f32)], axis=0
    ).T

    att_acc[...] = jnp.zeros_like(att_acc)
    qg_acc[...] = jnp.zeros_like(qg_acc)
    kg_acc[...] = jnp.zeros_like(kg_acc)
    vg_acc[...] = jnp.zeros_like(vg_acc)

    @pl.loop(0, row_count // chunk)
    def _(block):
        lines = pl.ds(pl.multiple_of(block * crows, crows), crows)
        first = (block * chunk).astype(f32)
        stats = stat_rows[pl.ds(pl.multiple_of(block * chunk, chunk), chunk), :]
        stats = jnp.broadcast_to(stats[:, None, :], (chunk, HEADS, 128)).reshape(crows, 128)
        factor = jnp.sum(jnp.where(lane_gap == 0.0, stats, 0.0), axis=1, keepdims=True)
        delta = jnp.sum(jnp.where(lane_gap == float(HEADS), stats, 0.0), axis=1, keepdims=True)
        probs = ebuf[lines, :] * factor
        probs_low = probs.astype(bf16)
        grad_low = (probs * (gpbuf[lines, :] - delta)).astype(bf16)
        glow[lines, :] = grad_low
        fold = one_hot(slot_token_t == line_query_t + first)
        att = (dot(probs_low, value) * hm[...]).astype(bf16)
        att_acc[...] += dot(fold, att)
        query_grad = (dot(grad_low, key) * (scale * hm[...])).astype(bf16)
        qg_acc[...] += dot(fold, query_grad)
        kg_acc[...] += dot_tn(grad_low, qd[lines, :])
        vg_acc[...] += dot_tn(probs_low, gd[lines, :])

    a_send[...] = att_acc[...].reshape(cols, padded, width).astype(bf16)
    q_send[...] = qg_acc[...].reshape(cols, padded, width).astype(bf16)
    key_side = dot(pick_keys_t, (kg_acc[...] * scale).astype(bf16))
    value_side = dot(pick_keys_t, vg_acc[...].astype(bf16))
    kv_send[:, 0] = key_side.reshape(rows, padded, width).astype(bf16)
    kv_send[:, 1] = value_side.reshape(rows, padded, width).astype(bf16)

    def kv_copy(b, slot):
        return pltpu.make_async_remote_copy(
            src_ref=kv_send.at[b],
            dst_ref=kv_recv.at[slot],
            send_sem=kv_sems.at[0, b],
            recv_sem=kv_sems.at[1, slot],
            device_id=device(col * rows + b),
            device_id_type=MESH,
        )

    def kv_start(b):
        pl.when(col * rows + b != me)(lambda: kv_copy(b, row).start())

    def kv_sent(b):
        pl.when(col * rows + b != me)(lambda: kv_copy(b, row).wait_send())

    def kv_wait(r):
        pl.when(r * cols + me // rows != me)(lambda: kv_copy(0, r).wait_recv())

    each(0, rows, kv_start)
    q_start()
    a_start()
    a_recv[col] = a_send[col]
    q_recv[col] = q_send[col]

    @pl.when(me // rows == col)
    def _():
        kv_recv[row] = kv_send[me % rows]

    bw_acc[...] = jnp.zeros_like(bw_acc)
    gain_acc[...] = jnp.zeros_like(gain_acc)

    def backward_row(i):
        grad_low = glow[pl.ds(pl.multiple_of(i * HEADS, HEADS), HEADS), :]
        norm = normed[i]
        grad_normed = dot_tn(grad_low, bw_t)
        bw_part = dot(grad_low, (norm * gain).astype(bf16))
        scaled = grad_normed * gain
        gain_part = grad_normed * norm
        along = jnp.mean(gain_part * gain, axis=1, keepdims=True)
        pair_grad[i] = (
            inv[i] * (scaled - jnp.mean(scaled, axis=1, keepdims=True) - norm * along)
        ).astype(bf16)
        return bw_part, gain_part

    def backward(first, last):
        @pl.loop(first // unroll, last // unroll)
        def _(block):
            bw_sum = bw_acc[...]
            gain_sum = gain_acc[...]
            for u in range(unroll):
                bw_part, gain_part = backward_row(block * unroll + u)
                bw_sum += bw_part
                gain_sum += gain_part
            bw_acc[...] = bw_sum
            gain_acc[...] = gain_sum

    split = (row_count // unroll // 2) * unroll
    backward(0, split)

    a_wait()
    q_wait()
    each(0, rows, kv_wait)
    att_own = a_recv[0].astype(f32)
    qg_own = q_recv[0].astype(f32)
    for k in range(1, cols):
        att_own += a_recv[k].astype(f32)
        qg_own += q_recv[k].astype(f32)
    kg_own = kv_recv[0, 0].astype(f32)
    vg_own = kv_recv[0, 1].astype(f32)
    for k in range(1, rows):
        kg_own += kv_recv[k, 0].astype(f32)
        vg_own += kv_recv[k, 1].astype(f32)
    qg_low = qg_own.astype(bf16)
    kg_low = kg_own.astype(bf16)
    vg_low = vg_own.astype(bf16)
    ag[me, 0] = qg_low
    ag[me, 1] = kg_low
    ag[me, 2] = vg_low
    ag[me, 3] = att_own.astype(bf16)
    ag_start()

    backward(split, row_count)
    fin[me, 0:HEADS] = bw_acc[...]
    fin[me, HEADS : HEADS + 8] = jnp.broadcast_to(
        jnp.sum(gain_acc[...], axis=0, keepdims=True), (8, channels)
    )
    fin_start()
    out_rows = dot_nt(qg_low, wq[...]) + dot_nt(kg_low, wk[...]) + dot_nt(vg_low, wv[...])
    single_grad[...] = out_rows[:own].astype(bf16)

    share = wgq.shape[0]
    share_pad = (share + 15) // 16 * 16
    pick = one_hot(
        iota((share_pad, width), 1)
        == iota((share_pad, width), 0) + (me * share).astype(f32)
    )
    tokens_t = dot_nt(pick, sbuf[...].reshape(group * padded, width)).astype(bf16)
    g_recv()
    ag_pass()
    ag_recv()
    for k, out in enumerate((wgq, wgk, wgv)):
        out[...] = dot(tokens_t, ag[:, k].reshape(group * padded, width))[:share]
    att_t = dot_nt(pick, ag[:, 3].reshape(group * padded, width)).astype(bf16)
    wgo[...] = dot(att_t, gbuf[...].reshape(group * padded, width))[:share]

    fin_recv()
    total_parts = fin[0]
    for k in range(1, group):
        total_parts += fin[k]
    bwg[...] = total_parts[0:HEADS]
    gg[...] = total_parts[HEADS : HEADS + 1]
    s_sent()
    g_sent()
    st_sent()
    a_sent()
    q_sent()
    each(0, rows, kv_sent)
    ag_sent()
    fin_sent()


def store(*refs):
    sources, targets, held = refs[:8], refs[8:16], refs[16:24]
    load_sems, store_sems = refs[24:]
    loads = [
        pltpu.make_async_copy(sources[k], held[k], load_sems.at[k]) for k in range(8)
    ]
    stores = [
        pltpu.make_async_copy(held[k], targets[k], store_sems.at[k]) for k in range(8)
    ]
    for load in loads:
        load.start()
    for load, copy in zip(loads, stores):
        load.wait()
        copy.start()
    for copy in stores:
        copy.wait()


def body(rows, cols, pair, pair_gain, bias_weight, single, w_query, w_key, w_value, w_out, key_mask, out_grad):
    row_count, col_count, channels = pair.shape
    own, width = single.shape
    group = rows * cols
    padded = (own + 15) // 16 * 16
    lines = row_count * HEADS
    share = width // group
    chunk = 16 if row_count % 16 == 0 else 8 if row_count % 8 == 0 else row_count
    vmem = pl.BlockSpec(memory_space=pltpu.VMEM)
    hbm = pl.BlockSpec(memory_space=pltpu.HBM)
    shape = jax.ShapeDtypeStruct
    outs = pl.pallas_call(
        functools.partial(kernel, rows, cols),
        out_shape=(
            shape(pair.shape, bf16),
            shape(single.shape, bf16),
            shape((share, width), f32),
            shape((share, width), f32),
            shape((share, width), f32),
            shape((share, width), f32),
            shape((HEADS, channels), f32),
            shape((1, channels), f32),
        ),
        in_specs=[hbm] * 10,
        out_specs=(vmem,) * 8,
        scratch_shapes=[
            pltpu.VMEM((group, padded, width), bf16),
            pltpu.VMEM((group, padded, width), bf16),
            pltpu.VMEM((cols, 3 * HEADS, row_count), f32),
            pltpu.VMEM((cols, padded, width), bf16),
            pltpu.VMEM((cols, padded, width), bf16),
            pltpu.VMEM((cols, padded, width), bf16),
            pltpu.VMEM((cols, padded, width), bf16),
            pltpu.VMEM((rows, 2, padded, width), bf16),
            pltpu.VMEM((rows, 2, padded, width), bf16),
            pltpu.VMEM((group, 4, padded, width), bf16),
            pltpu.VMEM((group, HEADS + 8, channels), f32),
            pltpu.VMEM((row_count, col_count, channels), f32),
            pltpu.VMEM((row_count, col_count, 1), f32),
            pltpu.VMEM((lines, col_count), f32),
            pltpu.VMEM((lines, col_count), f32),
            pltpu.VMEM((16, 128), bf16),
            pltpu.VMEM((lines, col_count), bf16),
            pltpu.VMEM((lines, width), bf16),
            pltpu.VMEM((lines, width), bf16),
            pltpu.VMEM((chunk * HEADS, width), f32),
            pltpu.VMEM((row_count, 128), f32),
            pltpu.VMEM((cols * padded, width), f32),
            pltpu.VMEM((cols * padded, width), f32),
            pltpu.VMEM((col_count, width), f32),
            pltpu.VMEM((col_count, width), f32),
            pltpu.VMEM((HEADS, channels), f32),
            pltpu.VMEM((col_count, channels), f32),
            pltpu.SemaphoreType.DMA((2, group)),
            pltpu.SemaphoreType.DMA((2, cols)),
            pltpu.SemaphoreType.DMA((2, cols)),
            pltpu.SemaphoreType.DMA((2, cols)),
            pltpu.SemaphoreType.DMA((2, rows)),
            pltpu.SemaphoreType.DMA((2, cols)),
            pltpu.SemaphoreType.DMA((2, cols)),
            pltpu.SemaphoreType.DMA((2, cols)),
            pltpu.SemaphoreType.DMA((2, rows, cols)),
            pltpu.SemaphoreType.DMA((2, rows, cols)),
            pltpu.SemaphoreType.DMA((2, rows, cols)),
            pltpu.VMEM(pair.shape, bf16),
            pltpu.VMEM((1, channels), f32),
            pltpu.VMEM((HEADS, channels), bf16),
            pltpu.VMEM(single.shape, bf16),
            pltpu.VMEM(w_query.shape, bf16),
            pltpu.VMEM(w_key.shape, bf16),
            pltpu.VMEM(w_value.shape, bf16),
            pltpu.VMEM(w_out.shape, bf16),
            pltpu.VMEM((1, col_count), jnp.int32),
            pltpu.VMEM(out_grad.shape, bf16),
            pltpu.SemaphoreType.DMA((10,)),
        ],
        compiler_params=pltpu.CompilerParams(
            collective_id=0, has_side_effects=True, vmem_limit_bytes=64 * 1024 * 1024
        ),
    )(
        pair,
        pair_gain.reshape(1, channels),
        bias_weight.T,
        single,
        w_query,
        w_key,
        w_value,
        w_out,
        key_mask.reshape(1, col_count),
        out_grad,
    )
    outs = pl.pallas_call(
        store,
        out_shape=tuple(shape(out.shape, out.dtype) for out in outs),
        in_specs=[pl.BlockSpec(memory_space=pl.ANY)] * 8,
        out_specs=(hbm,) * 8,
        scratch_shapes=[pltpu.VMEM(out.shape, out.dtype) for out in outs]
        + [pltpu.SemaphoreType.DMA((8,)), pltpu.SemaphoreType.DMA((8,))],
        compiler_params=pltpu.CompilerParams(vmem_limit_bytes=64 * 1024 * 1024),
    )(*outs)
    return outs[:-2] + (outs[-2].T, outs[-1].reshape(channels))


def solution(mesh):
    tokens = ("sample", "row", "col")
    in_specs = (
        P(("sample", "row"), "col", None),
        P(),
        P(),
        P(tokens, None),
        P(),
        P(),
        P(),
        P(),
        P(("sample", "col")),
        P(tokens, None),
    )
    out_specs = (
        P(("sample", "row"), "col", None),
        P(tokens, None),
        P(tokens, None),
        P(tokens, None),
        P(tokens, None),
        P(tokens, None),
        P("sample", None),
        P("sample"),
    )
    return jax.shard_map(
        functools.partial(body, mesh.shape["row"], mesh.shape["col"]),
        mesh=mesh,
        in_specs=in_specs,
        out_specs=out_specs,
        check_vma=False,
    )
```

```python
import functools

import jax
import jax.numpy as jnp
from jax import lax
from jax.experimental import pallas as pl
from jax.experimental.pallas import tpu as pltpu
from jax.sharding import PartitionSpec as P

HEADS = 16
HEAD = 24

norm_eps = 1e-05
masked_score = -1000000000.0
f32 = jnp.float32
bf16 = jnp.bfloat16
MESH = pl.DeviceIdType.MESH


def dot(a, b, contract=((1,), (0,))):
    return lax.dot_general(a, b, (contract, ((), ())), preferred_element_type=f32)


def dot_nt(a, b):
    return dot(a, b, ((1,), (1,)))


def dot_tn(a, b):
    return dot(a, b, ((0,), (0,)))


def iota(shape, dim):
    return lax.broadcasted_iota(jnp.int32, shape, dim).astype(f32)


def whole(x, unit):
    return jnp.floor((x + 0.5) * (1.0 / unit))


def one_hot(condition):
    return jnp.where(condition, 1.0, 0.0).astype(bf16)


def each(first, last, step):
    if last - first <= 16:
        for k in range(first, last):
            step(k)
    else:
        pl.loop(first, last)(step)


def kernel(
    rows,
    cols,
    pair_hbm,
    gain_hbm,
    bw_hbm,
    single_hbm,
    wq_hbm,
    wk_hbm,
    wv_hbm,
    wo_hbm,
    mask_hbm,
    og_hbm,
    pair_grad,
    single_grad,
    wgq,
    wgk,
    wgv,
    wgo,
    bwg,
    gg,
    sbuf,
    gbuf,
    stat,
    a_send,
    a_recv,
    q_send,
    q_recv,
    kv_send,
    kv_recv,
    ag,
    fin,
    normed,
    inv,
    ebuf,
    gpbuf,
    glow,
    qd,
    gd,
    hm,
    stat_rows,
    att_acc,
    qg_acc,
    kg_acc,
    vg_acc,
    bw_acc,
    gain_acc,
    sems,
    stat_sems,
    a_sems,
    q_sems,
    kv_sems,
    s_sems,
    g_sems,
    ag_sems,
    s_row_sems,
    g_row_sems,
    ag_row_sems,
    pair,
    gain_ref,
    bw,
    single,
    wq,
    wk,
    wv,
    wo,
    mask_ref,
    og,
    in_sems,
):
    group = rows * cols
    own, width = single.shape
    padded = sbuf.shape[1]
    row_count, col_count, channels = pair.shape
    row = lax.axis_index("row")
    col = lax.axis_index("col")
    me = row * cols + col
    scale = HEAD ** (-0.5)
    chunk = 16 if row_count % 16 == 0 else 8 if row_count % 8 == 0 else row_count
    crows = chunk * HEADS
    pad_rows = cols * padded
    pad_cols = rows * padded

    def device(index):
        return {"row": index // cols, "col": index % cols}

    def peer(k):
        return lax.rem(me + k, group)

    def sender(k):
        return lax.rem(me + group - k, group)

    loads = [
        pltpu.make_async_copy(source, target, in_sems.at[k])
        for k, (source, target) in enumerate(
            (
                (single_hbm, single),
                (og_hbm, og),
                (gain_hbm, gain_ref),
                (bw_hbm, bw),
                (pair_hbm, pair),
                (wq_hbm, wq),
                (wk_hbm, wk),
                (wv_hbm, wv),
                (wo_hbm, wo),
                (mask_hbm, mask_ref),
            )
        )
    ]
    barrier = pltpu.get_barrier_semaphore()

    def greet(k):
        pl.semaphore_signal(barrier, inc=1, device_id=device(peer(k)), device_id_type=MESH)

    each(1, group, greet)
    for load in loads:
        load.start()

    def gather(buf, kind):
        def direct(k, slot):
            return pltpu.make_async_remote_copy(
                src_ref=buf.at[me],
                dst_ref=buf.at[slot],
                send_sem=sems.at[2 * kind, k],
                recv_sem=sems.at[2 * kind + 1, k],
                device_id=device(peer(k)),
                device_id_type=MESH,
            )

        return (
            lambda: each(1, group, lambda k: direct(k, me).start()),
            lambda: each(1, group, lambda k: direct(k, sender(k)).wait_recv()),
            lambda: each(1, group, lambda k: direct(k, me).wait_send()),
        )

    def gather_two(buf, col_sems, row_sems):
        def across(k, slot):
            return pltpu.make_async_remote_copy(
                src_ref=buf.at[me],
                dst_ref=buf.at[slot],
                send_sem=col_sems.at[0, k],
                recv_sem=col_sems.at[1, k],
                device_id={"row": row, "col": lax.rem(col + k, cols)},
                device_id_type=MESH,
            )

        def relay(j, k, slot_row):
            place = lax.rem(col + cols - k, cols)
            return pltpu.make_async_remote_copy(
                src_ref=buf.at[row * cols + place],
                dst_ref=buf.at[slot_row * cols + place],
                send_sem=row_sems.at[0, j, k],
                recv_sem=row_sems.at[1, j, k],
                device_id={"row": lax.rem(row + j, rows), "col": col},
                device_id_type=MESH,
            )

        def start():
            each(1, cols, lambda k: across(k, me).start())
            each(1, rows, lambda j: relay(j, 0, row).start())

        def pass_on():
            def one(k):
                across(k, row * cols + lax.rem(col + cols - k, cols)).wait_recv()
                each(1, rows, lambda j: relay(j, k, row).start())

            each(1, cols, one)

        def receive():
            def one(j):
                slot_row = lax.rem(row + rows - j, rows)
                each(0, cols, lambda k: relay(j, k, slot_row).wait_recv())

            each(1, rows, one)

        def sent():
            each(1, cols, lambda k: across(k, me).wait_send())
            each(1, rows, lambda j: each(0, cols, lambda k: relay(j, k, row).wait_send()))

        return start, pass_on, receive, sent

    def along_col(src_of, buf, col_sems):
        def copy(k, slot):
            target = lax.rem(col + k, cols)
            return pltpu.make_async_remote_copy(
                src_ref=src_of(target),
                dst_ref=buf.at[slot],
                send_sem=col_sems.at[0, k],
                recv_sem=col_sems.at[1, k],
                device_id={"row": row, "col": target},
                device_id_type=MESH,
            )

        return (
            lambda: each(1, cols, lambda k: copy(k, col).start()),
            lambda: each(
                1, cols, lambda k: copy(k, lax.rem(col + cols - k, cols)).wait_recv()
            ),
            lambda: each(1, cols, lambda k: copy(k, col).wait_send()),
        )

    s_start, s_pass, s_recv, s_sent = gather_two(sbuf, s_sems, s_row_sems)
    g_start, g_pass, g_recv, g_sent = gather_two(gbuf, g_sems, g_row_sems)
    ag_start, ag_pass, ag_recv, ag_sent = gather_two(ag, ag_sems, ag_row_sems)
    fin_start, fin_recv, fin_sent = gather(fin, 0)
    st_start, st_recv, st_sent = along_col(lambda target: stat.at[col], stat, stat_sems)
    a_start, a_wait, a_sent = along_col(lambda target: a_send.at[target], a_recv, a_sems)
    q_start, q_wait, q_sent = along_col(lambda target: q_send.at[target], q_recv, q_sems)

    loads[0].wait()
    loads[1].wait()
    pad_own = one_hot(iota((padded, own), 0) == iota((padded, own), 1))
    sbuf[me] = dot(pad_own, single[...]).astype(bf16)
    gbuf[me] = dot(pad_own, og[...]).astype(bf16)
    pl.semaphore_wait(barrier, group - 1)
    s_start()
    g_start()

    for load in loads[2:5]:
        load.wait()
    gain = gain_ref[...]
    bw_t = bw[...]

    def forward_row(i):
        x = pair[i].astype(f32)
        centred = x - jnp.mean(x, axis=1, keepdims=True)
        inverse = lax.rsqrt(jnp.mean(centred * centred, axis=1, keepdims=True) + norm_eps)
        norm = centred * inverse
        normed[i] = norm
        inv[i] = inverse
        ebuf[pl.ds(pl.multiple_of(i * HEADS, HEADS), HEADS), :] = dot_nt(
            bw_t, (norm * gain).astype(bf16)
        )

    unroll = 8 if row_count % 8 == 0 else 1

    split = (row_count // unroll // 2) * unroll

    def forward(first, last):
        @pl.loop(first // unroll, last // unroll)
        def _(block):
            for u in range(unroll):
                forward_row(block * unroll + u)

    forward(0, split)
    s_pass()
    forward(split, row_count)

    line = iota((crows, 1), 0)
    line_query = whole(line, HEADS)
    line_head = line - line_query * HEADS
    hm[...] = jnp.where(whole(iota((1, width), 1), HEAD) == line_head, 1.0, 0.0)
    lane_gap = iota((1, 128), 1) - line_head
    slot_of = iota((1, pad_rows), 1)
    slot_in = slot_of - whole(slot_of, padded) * padded
    slot_token = jnp.where(slot_in < own, whole(slot_of, padded) * own + slot_in, -1.0)
    slot_of_t = iota((pad_rows, 1), 0)
    slot_in_t = slot_of_t - whole(slot_of_t, padded) * padded
    slot_token_t = jnp.where(
        slot_in_t < own, whole(slot_of_t, padded) * own + slot_in_t, -1.0
    )
    line_query_t = whole(iota((1, crows), 1), HEADS)
    key_slot = iota((1, pad_cols), 1)
    key_in = key_slot - whole(key_slot, padded) * padded
    key_token = jnp.where(key_in < own, whole(key_slot, padded) * own + key_in, -1.0)
    key_slot_t = iota((pad_cols, 1), 0)
    key_in_t = key_slot_t - whole(key_slot_t, padded) * padded
    key_token_t = jnp.where(key_in_t < own, whole(key_slot_t, padded) * own + key_in_t, -1.0)
    pick_keys = one_hot(key_token == iota((col_count, 1), 0))
    pick_keys_t = one_hot(key_token_t == iota((1, col_count), 1))

    for load in loads[5:]:
        load.wait()
    s_recv()
    row_tokens = sbuf[pl.ds(row * cols, cols)].reshape(pad_rows, width)
    col_tokens = sbuf[pl.ds(col * rows, rows)].reshape(pad_cols, width)
    query = dot(row_tokens, wq[...]).astype(bf16)
    key = dot(pick_keys, dot(col_tokens, wk[...]).astype(bf16)).astype(bf16)
    value = dot(pick_keys, dot(col_tokens, wv[...]).astype(bf16)).astype(bf16)
    g_pass()
    grad_tokens = gbuf[pl.ds(row * cols, cols)].reshape(pad_rows, width)
    grad_att = dot_nt(grad_tokens, wo[...]).astype(bf16)
    live = mask_ref[...] > 0

    @pl.loop(0, row_count // chunk)
    def _(block):
        lines = pl.ds(pl.multiple_of(block * crows, crows), crows)
        first = (block * chunk).astype(f32)
        spread = one_hot(slot_token == line_query + first)
        q_diag = (dot(spread, query) * hm[...]).astype(bf16)
        g_diag = (dot(spread, grad_att) * hm[...]).astype(bf16)
        qd[lines, :] = q_diag
        gd[lines, :] = g_diag
        scores = dot_nt(q_diag, key) * scale + ebuf[lines, :]
        scores = jnp.where(live, scores, masked_score)
        top = jnp.max(scores, axis=1, keepdims=True)
        exps = jnp.exp(scores - top)
        grad_probs = dot_nt(g_diag, value)
        total = jnp.sum(exps, axis=1, keepdims=True)
        part = jnp.sum(exps * grad_probs, axis=1, keepdims=True)
        ebuf[lines, :] = exps
        gpbuf[lines, :] = grad_probs
        placed = jnp.where(
            lane_gap == 0.0,
            top,
            jnp.where(
                lane_gap == float(HEADS), total, jnp.where(lane_gap == 2.0 * HEADS, part, 0.0)
            ),
        )
        stat_rows[pl.ds(pl.multiple_of(block * chunk, chunk), chunk), :] = jnp.sum(
            placed.reshape(chunk, HEADS, 128), axis=1
        )

    stat[col] = stat_rows[...].T[: 3 * HEADS]
    st_start()
    st_recv()
    own_top = stat[col, 0:HEADS]
    row_top = stat[0, 0:HEADS]
    for k in range(1, cols):
        row_top = jnp.maximum(row_top, stat[k, 0:HEADS])
    row_total = jnp.zeros_like(row_top)
    delta = jnp.zeros_like(row_top)
    for k in range(cols):
        weight = jnp.exp(stat[k, 0:HEADS] - row_top)
        row_total += weight * stat[k, HEADS : 2 * HEADS]
        delta += weight * stat[k, 2 * HEADS : 3 * HEADS]
    factor = jnp.exp(own_top - row_top) / row_total
    delta = delta / row_total
    stat_rows[...] = jnp.concatenate(
        [factor, delta, jnp.zeros((128 - 2 * HEADS, row_count), f32)], axis=0
    ).T

    att_acc[...] = jnp.zeros_like(att_acc)
    qg_acc[...] = jnp.zeros_like(qg_acc)
    kg_acc[...] = jnp.zeros_like(kg_acc)
    vg_acc[...] = jnp.zeros_like(vg_acc)

    @pl.loop(0, row_count // chunk)
    def _(block):
        lines = pl.ds(pl.multiple_of(block * crows, crows), crows)
        first = (block * chunk).astype(f32)
        stats = stat_rows[pl.ds(pl.multiple_of(block * chunk, chunk), chunk), :]
        stats = jnp.broadcast_to(stats[:, None, :], (chunk, HEADS, 128)).reshape(crows, 128)
        factor = jnp.sum(jnp.where(lane_gap == 0.0, stats, 0.0), axis=1, keepdims=True)
        delta = jnp.sum(jnp.where(lane_gap == float(HEADS), stats, 0.0), axis=1, keepdims=True)
        probs = ebuf[lines, :] * factor
        probs_low = probs.astype(bf16)
        grad_low = (probs * (gpbuf[lines, :] - delta)).astype(bf16)
        glow[lines, :] = grad_low
        fold = one_hot(slot_token_t == line_query_t + first)
        att = (dot(probs_low, value) * hm[...]).astype(bf16)
        att_acc[...] += dot(fold, att)
        query_grad = (dot(grad_low, key) * (scale * hm[...])).astype(bf16)
        qg_acc[...] += dot(fold, query_grad)
        kg_acc[...] += dot_tn(grad_low, qd[lines, :])
        vg_acc[...] += dot_tn(probs_low, gd[lines, :])

    a_send[...] = att_acc[...].reshape(cols, padded, width).astype(bf16)
    q_send[...] = qg_acc[...].reshape(cols, padded, width).astype(bf16)
    key_side = dot(pick_keys_t, (kg_acc[...] * scale).astype(bf16))
    value_side = dot(pick_keys_t, vg_acc[...].astype(bf16))
    kv_send[:, 0] = key_side.reshape(rows, padded, width).astype(bf16)
    kv_send[:, 1] = value_side.reshape(rows, padded, width).astype(bf16)

    def kv_copy(b, slot):
        return pltpu.make_async_remote_copy(
            src_ref=kv_send.at[b],
            dst_ref=kv_recv.at[slot],
            send_sem=kv_sems.at[0, b],
            recv_sem=kv_sems.at[1, slot],
            device_id=device(col * rows + b),
            device_id_type=MESH,
        )

    def kv_start(b):
        pl.when(col * rows + b != me)(lambda: kv_copy(b, row).start())

    def kv_sent(b):
        pl.when(col * rows + b != me)(lambda: kv_copy(b, row).wait_send())

    def kv_wait(r):
        pl.when(r * cols + me // rows != me)(lambda: kv_copy(0, r).wait_recv())

    each(0, rows, kv_start)
    q_start()
    a_start()
    a_recv[col] = a_send[col]
    q_recv[col] = q_send[col]

    @pl.when(me // rows == col)
    def _():
        kv_recv[row] = kv_send[me % rows]

    bw_acc[...] = jnp.zeros_like(bw_acc)
    gain_acc[...] = jnp.zeros_like(gain_acc)

    def backward_row(i):
        grad_low = glow[pl.ds(pl.multiple_of(i * HEADS, HEADS), HEADS), :]
        norm = normed[i]
        grad_normed = dot_tn(grad_low, bw_t)
        bw_part = dot(grad_low, (norm * gain).astype(bf16))
        scaled = grad_normed * gain
        gain_part = grad_normed * norm
        along = jnp.mean(gain_part * gain, axis=1, keepdims=True)
        pair_grad[i] = (
            inv[i] * (scaled - jnp.mean(scaled, axis=1, keepdims=True) - norm * along)
        ).astype(bf16)
        return bw_part, gain_part

    def backward(first, last):
        @pl.loop(first // unroll, last // unroll)
        def _(block):
            bw_sum = bw_acc[...]
            gain_sum = gain_acc[...]
            for u in range(unroll):
                bw_part, gain_part = backward_row(block * unroll + u)
                bw_sum += bw_part
                gain_sum += gain_part
            bw_acc[...] = bw_sum
            gain_acc[...] = gain_sum

    backward(0, split)

    a_wait()
    q_wait()
    each(0, rows, kv_wait)
    att_own = a_recv[0].astype(f32)
    qg_own = q_recv[0].astype(f32)
    for k in range(1, cols):
        att_own += a_recv[k].astype(f32)
        qg_own += q_recv[k].astype(f32)
    kg_own = kv_recv[0, 0].astype(f32)
    vg_own = kv_recv[0, 1].astype(f32)
    for k in range(1, rows):
        kg_own += kv_recv[k, 0].astype(f32)
        vg_own += kv_recv[k, 1].astype(f32)
    qg_low = qg_own.astype(bf16)
    kg_low = kg_own.astype(bf16)
    vg_low = vg_own.astype(bf16)
    ag[me, 0] = qg_low
    ag[me, 1] = kg_low
    ag[me, 2] = vg_low
    ag[me, 3] = att_own.astype(bf16)
    ag_start()

    backward(split, row_count)
    fin[me, 0:HEADS] = bw_acc[...]
    fin[me, HEADS : HEADS + 8] = jnp.broadcast_to(
        jnp.sum(gain_acc[...], axis=0, keepdims=True), (8, channels)
    )
    fin_start()
    out_rows = dot_nt(qg_low, wq[...]) + dot_nt(kg_low, wk[...]) + dot_nt(vg_low, wv[...])
    single_grad[...] = out_rows[:own].astype(bf16)

    share = wgq.shape[0]
    share_pad = (share + 15) // 16 * 16
    pick = one_hot(
        iota((share_pad, width), 1)
        == iota((share_pad, width), 0) + (me * share).astype(f32)
    )
    tokens_t = dot_nt(pick, sbuf[...].reshape(group * padded, width)).astype(bf16)
    g_recv()
    ag_pass()
    ag_recv()
    for k, out in enumerate((wgq, wgk, wgv)):
        out[...] = dot(tokens_t, ag[:, k].reshape(group * padded, width))[:share]
    att_t = dot_nt(pick, ag[:, 3].reshape(group * padded, width)).astype(bf16)
    wgo[...] = dot(att_t, gbuf[...].reshape(group * padded, width))[:share]

    fin_recv()
    total_parts = fin[0]
    for k in range(1, group):
        total_parts += fin[k]
    bwg[...] = total_parts[0:HEADS]
    gg[...] = total_parts[HEADS : HEADS + 1]
    s_sent()
    g_sent()
    st_sent()
    a_sent()
    q_sent()
    each(0, rows, kv_sent)
    ag_sent()
    fin_sent()


def store(*refs):
    sources, targets, held = refs[:8], refs[8:16], refs[16:24]
    load_sems, store_sems = refs[24:]
    loads = [
        pltpu.make_async_copy(sources[k], held[k], load_sems.at[k]) for k in range(8)
    ]
    stores = [
        pltpu.make_async_copy(held[k], targets[k], store_sems.at[k]) for k in range(8)
    ]
    for load in loads:
        load.start()
    for load, copy in zip(loads, stores):
        load.wait()
        copy.start()
    for copy in stores:
        copy.wait()


def body(rows, cols, pair, pair_gain, bias_weight, single, w_query, w_key, w_value, w_out, key_mask, out_grad):
    row_count, col_count, channels = pair.shape
    own, width = single.shape
    group = rows * cols
    padded = (own + 15) // 16 * 16
    lines = row_count * HEADS
    share = width // group
    chunk = 16 if row_count % 16 == 0 else 8 if row_count % 8 == 0 else row_count
    vmem = pl.BlockSpec(memory_space=pltpu.VMEM)
    hbm = pl.BlockSpec(memory_space=pltpu.HBM)
    shape = jax.ShapeDtypeStruct
    outs = pl.pallas_call(
        functools.partial(kernel, rows, cols),
        out_shape=(
            shape(pair.shape, bf16),
            shape(single.shape, bf16),
            shape((share, width), f32),
            shape((share, width), f32),
            shape((share, width), f32),
            shape((share, width), f32),
            shape((HEADS, channels), f32),
            shape((1, channels), f32),
        ),
        in_specs=[hbm] * 10,
        out_specs=(vmem,) * 8,
        scratch_shapes=[
            pltpu.VMEM((group, padded, width), bf16),
            pltpu.VMEM((group, padded, width), bf16),
            pltpu.VMEM((cols, 3 * HEADS, row_count), f32),
            pltpu.VMEM((cols, padded, width), bf16),
            pltpu.VMEM((cols, padded, width), bf16),
            pltpu.VMEM((cols, padded, width), bf16),
            pltpu.VMEM((cols, padded, width), bf16),
            pltpu.VMEM((rows, 2, padded, width), bf16),
            pltpu.VMEM((rows, 2, padded, width), bf16),
            pltpu.VMEM((group, 4, padded, width), bf16),
            pltpu.VMEM((group, HEADS + 8, channels), f32),
            pltpu.VMEM((row_count, col_count, channels), f32),
            pltpu.VMEM((row_count, col_count, 1), f32),
            pltpu.VMEM((lines, col_count), f32),
            pltpu.VMEM((lines, col_count), f32),
            pltpu.VMEM((lines, col_count), bf16),
            pltpu.VMEM((lines, width), bf16),
            pltpu.VMEM((lines, width), bf16),
            pltpu.VMEM((chunk * HEADS, width), f32),
            pltpu.VMEM((row_count, 128), f32),
            pltpu.VMEM((cols * padded, width), f32),
            pltpu.VMEM((cols * padded, width), f32),
            pltpu.VMEM((col_count, width), f32),
            pltpu.VMEM((col_count, width), f32),
            pltpu.VMEM((HEADS, channels), f32),
            pltpu.VMEM((col_count, channels), f32),
            pltpu.SemaphoreType.DMA((2, group)),
            pltpu.SemaphoreType.DMA((2, cols)),
            pltpu.SemaphoreType.DMA((2, cols)),
            pltpu.SemaphoreType.DMA((2, cols)),
            pltpu.SemaphoreType.DMA((2, rows)),
            pltpu.SemaphoreType.DMA((2, cols)),
            pltpu.SemaphoreType.DMA((2, cols)),
            pltpu.SemaphoreType.DMA((2, cols)),
            pltpu.SemaphoreType.DMA((2, rows, cols)),
            pltpu.SemaphoreType.DMA((2, rows, cols)),
            pltpu.SemaphoreType.DMA((2, rows, cols)),
            pltpu.VMEM(pair.shape, bf16),
            pltpu.VMEM((1, channels), f32),
            pltpu.VMEM((HEADS, channels), bf16),
            pltpu.VMEM(single.shape, bf16),
            pltpu.VMEM(w_query.shape, bf16),
            pltpu.VMEM(w_key.shape, bf16),
            pltpu.VMEM(w_value.shape, bf16),
            pltpu.VMEM(w_out.shape, bf16),
            pltpu.VMEM((1, col_count), jnp.int32),
            pltpu.VMEM(out_grad.shape, bf16),
            pltpu.SemaphoreType.DMA((10,)),
        ],
        compiler_params=pltpu.CompilerParams(
            collective_id=0, has_side_effects=True, vmem_limit_bytes=64 * 1024 * 1024
        ),
    )(
        pair,
        pair_gain.reshape(1, channels),
        bias_weight.T,
        single,
        w_query,
        w_key,
        w_value,
        w_out,
        key_mask.reshape(1, col_count),
        out_grad,
    )
    outs = pl.pallas_call(
        store,
        out_shape=tuple(shape(out.shape, out.dtype) for out in outs),
        in_specs=[pl.BlockSpec(memory_space=pl.ANY)] * 8,
        out_specs=(hbm,) * 8,
        scratch_shapes=[pltpu.VMEM(out.shape, out.dtype) for out in outs]
        + [pltpu.SemaphoreType.DMA((8,)), pltpu.SemaphoreType.DMA((8,))],
        compiler_params=pltpu.CompilerParams(vmem_limit_bytes=64 * 1024 * 1024),
    )(*outs)
    return outs[:-2] + (outs[-2].T, outs[-1].reshape(channels))


def solution(mesh):
    tokens = ("sample", "row", "col")
    in_specs = (
        P(("sample", "row"), "col", None),
        P(),
        P(),
        P(tokens, None),
        P(),
        P(),
        P(),
        P(),
        P(("sample", "col")),
        P(tokens, None),
    )
    out_specs = (
        P(("sample", "row"), "col", None),
        P(tokens, None),
        P(tokens, None),
        P(tokens, None),
        P(tokens, None),
        P(tokens, None),
        P("sample", None),
        P("sample"),
    )
    return jax.shard_map(
        functools.partial(body, mesh.shape["row"], mesh.shape["col"]),
        mesh=mesh,
        in_specs=in_specs,
        out_specs=out_specs,
        check_vma=False,
    )
```
